32 devices in a mesh: mirror: 2 (over y), rows: 4 (over z), cols: 4 (over x, core).
Axes of the slice: x: 2, y: 2, z: 4, core: 2. Of those that a mesh axis runs over, the one named last changes fastest.
Arguments:
- currents: bfloat16 [16, 131072], P(None, ('mirror', 'rows')), may hold values from -6 to 6
- right_side: float32 [16, 131072], P(None, ('mirror', 'rows', 'cols')), may hold values from -6 to 6
- geometry: float32 [4, 65536], replicated, may hold values from 0 to 4, as said below
Outputs:
- residual: float32 [16, 131072], P(None, ('mirror', 'rows', 'cols'))
- krylov_image: float32 [16, 131072], P(None, ('mirror', 'rows', 'cols'))
The draws below stay inside these ranges and needn't reach their ends.
Inputs may be any that keep to these rules, and one draw needn't show every extreme that they name: `geometry`: rows are x in [0, 1], y in [0.05, 0.45], z in [0, 4] and a size in [0.003, 0.03].
All inputs are finite; a program needn't handle non-finite values.
Results may differ from the reference program's by a relative error of at most 0.0024.
Values may be sent and summed in bfloat16 or wider, within the bound.
No kernel may reach another device: no remote copies, remote signals or barrier semaphores. Data moves between devices by JAX's collectives and lax.ppermute only.
A program may use at most 64 MiB of HBM per device.

```python
import math
import jax
import jax.numpy as jnp
from jax import lax

CELLS = 131072
HALF = 65536
RHS = 16


def draw_geometry(key, part):
    keys = jax.random.split(key, 4)
    across = jax.random.uniform(keys[0], (HALF,), jnp.float32, 0.0, 1.0)
    height = jax.random.uniform(keys[1], (HALF,), jnp.float32, 0.05, 0.45)
    depth = jax.random.uniform(keys[2], (HALF,), jnp.float32, 0.0, 4.0)
    log_size = jax.random.uniform(keys[3], (HALF,), jnp.float32, jnp.log(0.003), jnp.log(0.03))
    sizes = jnp.clip(jnp.exp(log_size), 0.003, 0.03)
    return jnp.stack([across, height, depth, sizes])


def levels(key, extent, shards, smallest, largest):
    def one(axis_at, shards_of):
        steps = jax.random.uniform(jax.random.fold_in(jax.random.fold_in(key, 6), axis_at), (shards_of,), jnp.float32, smallest / len(shards), largest / len(shards))
        return jnp.repeat(jnp.exp(steps), extent[axis_at] // shards_of).reshape((-1,) + (1,) * (len(extent) - axis_at - 1))

    gain = one(*shards[0])
    for cut in shards[1:]:
        gain = gain * one(*cut)
    return gain


def normal_values(stream_key, extent, deviation, limit, shards=(), held_as=jnp.bfloat16):
    values = jax.random.normal(stream_key, extent, jnp.float32) * deviation
    if len(shards) > 0:
        values = levels(stream_key, extent, shards, -0.22, 0.18) * values
    return jnp.clip(values, min=-limit, max=limit).astype(held_as)


def setup_inputs(seed: int = 0) -> dict:
    key_list = jax.random.split(jax.random.key(seed), 4)
    currents = normal_values(key_list[0], (RHS, CELLS), 1.0, 6.0, ((1, 8),))
    right_side = normal_values(key_list[1], (RHS, CELLS), 1.0, 6.0, ((1, 32),), jnp.float32)
    geometry = draw_geometry(jax.random.fold_in(key_list[3], 71), 0)
    return dict(currents=currents, right_side=right_side, geometry=geometry)


def kernel_block(row_geo, col_geo, reflect, scaling):
    diff_x = row_geo[0][:, None] - col_geo[0][None, :]
    diff_y = row_geo[1][:, None] - reflect * col_geo[1][None, :]
    diff_z = row_geo[2][:, None] - col_geo[2][None, :]
    spread = (row_geo[3] * row_geo[3])[:, None] + (col_geo[3] * col_geo[3])[None, :]
    squared = diff_x * diff_x + diff_y * diff_y + diff_z * diff_z + spread
    return (scaling / jnp.sqrt(squared)).astype(jnp.bfloat16)

def apply_operator(currents_in, geometry):
    scaling = 1.0 / math.sqrt(CELLS)
    first_cur = currents_in[:, :HALF].astype(jnp.float32)
    second_cur = currents_in[:, HALF:].astype(jnp.float32)
    block_len = min(512, HALF)
    block_count = HALF // block_len

    def one_block(position):
        offset = position * block_len
        geo_part = lax.dynamic_slice_in_dim(geometry, offset, block_len, 1)
        self_tile = kernel_block(geo_part, geometry, 1.0, scaling)
        mirror_tile = kernel_block(geo_part, geometry, -1.0, scaling)
        self_tile = lax.optimization_barrier(self_tile).astype(jnp.float32)
        mirror_tile = lax.optimization_barrier(mirror_tile).astype(jnp.float32)
        upper = jnp.dot(first_cur, self_tile.T, precision=lax.Precision.HIGHEST, preferred_element_type=jnp.float32) + jnp.dot(second_cur, mirror_tile.T, precision=lax.Precision.HIGHEST, preferred_element_type=jnp.float32)
        lower = jnp.dot(second_cur, self_tile.T, precision=lax.Precision.HIGHEST, preferred_element_type=jnp.float32) + jnp.dot(first_cur, mirror_tile.T, precision=lax.Precision.HIGHEST, preferred_element_type=jnp.float32)
        return (upper, lower)
    upper_all, lower_all = lax.map(one_block, jnp.arange(block_count, dtype=jnp.int32))
    excite = currents_in.shape[0]
    upper_all = jnp.transpose(upper_all, (1, 0, 2)).reshape(excite, HALF)
    lower_all = jnp.transpose(lower_all, (1, 0, 2)).reshape(excite, HALF)
    return jnp.concatenate([upper_all, lower_all], axis=1)

def reference(currents, right_side, geometry):
    voltage = apply_operator(currents, geometry)
    residual = right_side - voltage
    residual_b = residual.astype(jnp.bfloat16)
    krylov_image = apply_operator(residual_b, geometry)
    return (residual, krylov_image)
```

```python
import functools
import math

import jax
import jax.numpy as jnp
import numpy as np
from jax import lax
from jax.experimental import pallas as pl
from jax.experimental.pallas import tpu as pltpu
from jax.sharding import PartitionSpec as P

AXES = ("mirror", "rows", "cols")
F32 = jnp.float32
BF16 = jnp.bfloat16
SUB = 256
STRIP = 16
LAST = (((1,), (1,)), ((), ()))


class Plan:
    def __init__(self, pieces, half):
        self.pieces = pieces
        self.blocks = math.isqrt(4 * pieces)
        assert self.blocks * self.blocks == 4 * pieces and self.blocks % 4 == 0
        self.homes = self.blocks // 2
        self.per_half = pieces // self.blocks
        self.block_len = half // self.blocks
        self.piece_len = half // pieces
        self.tile = min(1024, self.block_len)
        self.tiles = self.block_len // self.tile

    def device(self, block, home):
        return home // self.per_half * self.pieces + block * self.per_half + home % self.per_half

    def route(self, near, step):
        pairs = []
        for block in range(self.blocks):
            for home in range(self.homes):
                other = block if near else (block + home + 1) % self.blocks
                source = self.device(other, (home + step) % self.homes)
                pairs.append((source, self.device(block, home)))
        return pairs

    def jobs(self):
        count = self.tiles
        pair = [(i, count + j) for i in range(count) for j in range(count)]
        diagonal = [
            (low + i, low + j) for low in (0, count) for i in range(count) for j in range(i + 1, count)
        ]
        tables = []
        for work in (pair, diagonal):
            table = np.zeros((3, count * count + 1), np.int32)
            for at, (i, j) in enumerate(work):
                table[:, at] = i, j, at == 0 or work[at - 1][0] != i
            tables.append(table)
        return tables[0], tables[1], len(pair), len(diagonal)


def operator_kernel(plan, table, counts, geo, *refs):
    pieces = refs[: plan.blocks]
    results = refs[plan.blocks : 2 * plan.blocks]
    drive, by_column, by_row, near, far, turned = refs[2 * plan.blocks :]
    tile, homes, piece_len = plan.tile, plan.homes, plan.piece_len
    chunks = tile // SUB
    strips = SUB // STRIP

    def place(index):
        home = lax.rem(counts[2] + index % homes, homes)
        half = home // plan.per_half
        offset = (index // homes) * plan.block_len + lax.rem(home, plan.per_half) * piece_len
        return half, pl.multiple_of(offset, 128)

    for index in range(plan.blocks):
        half, offset = place(index)
        value = pieces[index][...]
        drive[pl.ds(pl.multiple_of(half * 16, 16), 16), pl.ds(offset, piece_len)] = value
        drive[pl.ds(pl.multiple_of(48 - half * 16, 16), 16), pl.ds(offset, piece_len)] = value
    by_column[...] = jnp.zeros_like(by_column)
    by_row[...] = jnp.zeros_like(by_row)

    def turn(row0):
        for part in range(tile // 128):
            turned[part * 128 : part * 128 + 128, :] = jnp.transpose(geo[:, pl.ds(row0 + part * 128, 128)])

    def make(slot, row, col0, first, at, lanes=0):
        part = turned[row : row + STRIP, :]
        x_r, y_r, z_r, q_r = [jnp.broadcast_to(part[:, n : n + 1], (STRIP, 128)) for n in range(4)]
        for lane in range(lanes, tile, 128):
            cols = geo[:, pl.ds(col0 + lane, 128)]
            diff_x = x_r - cols[0:1]
            diff_z = z_r - cols[2:3]
            base = (q_r + cols[3:4]) + diff_x * diff_x + diff_z * diff_z
            cross = y_r * cols[4:5]
            near[slot, at : at + STRIP, lane : lane + 128] = lax.rsqrt(base - cross).astype(BF16)
            far[slot, at : at + STRIP, lane : lane + 128] = lax.rsqrt(base + cross).astype(BF16)

    def to_columns(slot, row0, col0, chunk):
        lanes = slice(chunk * SUB, chunk * SUB + SUB)
        rows = pl.ds(row0, SUB)
        by_column[:, pl.ds(col0 + chunk * SUB, SUB)] += jnp.dot(
            drive[0:32, rows], near[slot, :, lanes], preferred_element_type=F32
        ) + jnp.dot(drive[32:64, rows], far[slot, :, lanes], preferred_element_type=F32)

    def to_rows(slot, col0, chunk):
        lanes = slice(chunk * SUB, chunk * SUB + SUB)
        cols = pl.ds(col0 + chunk * SUB, SUB)
        return lax.dot_general(
            drive[0:32, cols], near[slot, :, lanes], LAST, preferred_element_type=F32
        ) + lax.dot_general(drive[32:64, cols], far[slot, :, lanes], LAST, preferred_element_type=F32)

    def pair_tile(at, carry):
        row0 = pl.multiple_of(table[0, at] * tile, tile)
        col0 = pl.multiple_of(table[1, at] * tile, tile)
        next0 = pl.multiple_of(table[1, at + 1] * tile, tile)

        @pl.when(table[2, at] == 1)
        def _():
            turn(row0)
            for strip in range(strips):
                make(0, strip * STRIP, col0, True, strip * STRIP)

        for sub in range(chunks):
            ahead, ahead0 = (sub + 1, col0) if sub + 1 < chunks else (0, next0)
            total = None
            for chunk in range(chunks):
                for strip in range(chunk * strips // chunks, (chunk + 1) * strips // chunks):
                    make((sub + 1) % 2, ahead * SUB + strip * STRIP, ahead0, False, strip * STRIP)
                to_columns(sub % 2, row0 + sub * SUB, col0, chunk)
                term = to_rows(sub % 2, col0, chunk)
                total = term if total is None else total + term
            by_row[:, pl.ds(row0 + sub * SUB, SUB)] += total
        return carry

    def diagonal_tile(at, carry):
        row0 = pl.multiple_of(at * tile, tile)
        turn(row0)
        for sub in range(chunks):
            slot = sub % 2
            for strip in range(strips):
                make(slot, sub * SUB + strip * STRIP, row0, False, strip * STRIP, sub * SUB)
            total = None
            for chunk in range(sub, chunks):
                to_columns(slot, row0 + sub * SUB, row0, chunk)
                if chunk > sub:
                    term = to_rows(slot, row0, chunk)
                    total = term if total is None else total + term
            if total is not None:
                by_row[:, pl.ds(row0 + sub * SUB, SUB)] += total
        return carry

    lax.fori_loop(0, counts[0], pair_tile, 0)
    lax.fori_loop(0, counts[1], diagonal_tile, 0)

    for index in range(plan.blocks):
        half, offset = place(index)
        rows = pl.ds(pl.multiple_of(half * 16, 16), 16)
        cols = pl.ds(offset, piece_len)
        results[index][...] = by_column[rows, cols] + by_row[rows, cols]


def apply_operator(plan, table, counts, geo, pieces):
    cells = 2 * plan.block_len
    vmem = pl.BlockSpec(memory_space=pltpu.VMEM)
    smem = pl.BlockSpec(memory_space=pltpu.SMEM)
    return pl.pallas_call(
        functools.partial(operator_kernel, plan),
        in_specs=[smem, smem, vmem] + [vmem] * plan.blocks,
        out_specs=[vmem] * plan.blocks,
        out_shape=[jax.ShapeDtypeStruct((16, plan.piece_len), F32)] * plan.blocks,
        scratch_shapes=[
            pltpu.VMEM((64, cells), BF16),
            pltpu.VMEM((32, cells), F32),
            pltpu.VMEM((32, cells), F32),
            pltpu.VMEM((2, SUB, plan.tile), BF16),
            pltpu.VMEM((2, SUB, plan.tile), BF16),
            pltpu.VMEM((plan.tile, 8), F32),
        ],
        compiler_params=pltpu.CompilerParams(vmem_limit_bytes=40 * 2**20),
        name="peec_pairs",
    )(table, counts, geo, *pieces)


def gather_pieces(plan, own):
    pieces = [own]
    for step in range(1, plan.homes):
        pieces.append(lax.ppermute(own, AXES, plan.route(True, step)))
    for step in range(plan.homes):
        pieces.append(lax.ppermute(own, AXES, plan.route(False, step)))
    return pieces


def return_pieces(plan, partials):
    total = partials[0]
    for index in range(1, plan.blocks):
        route = plan.route(index < plan.homes, index % plan.homes)
        back = [(target, source) for source, target in route]
        total = total + lax.ppermute(partials[index], AXES, back)
    return total


def local_geometry(plan, geometry, block, partner):
    scale = math.sqrt(2 * geometry.shape[1])
    length = plan.block_len
    cells = jnp.concatenate(
        [lax.dynamic_slice_in_dim(geometry, at * length, length, 1) for at in (block, partner)], axis=1
    )
    x, y, z, size = [cells[n] * scale for n in range(4)]
    zero = jnp.zeros_like(x)
    return jnp.stack([x, y, z, y * y + size * size, y + y, zero, zero, zero])


def on_device(plan, currents, right_side, geometry):
    piece = lax.axis_index("rows") * lax.axis_size("cols") + lax.axis_index("cols")
    block = piece // plan.per_half
    home = lax.axis_index("mirror") * plan.per_half + piece % plan.per_half
    partner = (block + home + 1) % plan.blocks
    pair, diagonal, pair_count, diagonal_count = plan.jobs()
    on_diagonal = (home == plan.homes - 1) & (block >= plan.homes)
    table = jnp.where(on_diagonal, diagonal, pair)
    counts = jnp.stack(
        [
            jnp.where(on_diagonal, diagonal_count, pair_count),
            jnp.where(on_diagonal, 2 * plan.tiles, 0),
            home,
        ]
    ).astype(jnp.int32)
    geo = local_geometry(plan, geometry, block, partner)

    own = lax.dynamic_slice_in_dim(currents, lax.axis_index("cols") * plan.piece_len, plan.piece_len, 1)
    partials = apply_operator(plan, table, counts, geo, gather_pieces(plan, own))
    residual = right_side - return_pieces(plan, partials)
    partials = apply_operator(plan, table, counts, geo, gather_pieces(plan, residual.astype(BF16)))
    return residual, return_pieces(plan, partials)


def solution(mesh):
    pieces = mesh.shape["rows"] * mesh.shape["cols"]

    def whole(currents, right_side, geometry):
        plan = Plan(pieces, geometry.shape[1])
        return jax.shard_map(
            functools.partial(on_device, plan),
            mesh=mesh,
            in_specs=(P(None, ("mirror", "rows")), P(None, AXES), P()),
            out_specs=(P(None, AXES), P(None, AXES)),
            check_vma=False,
        )(currents, right_side, geometry)

    return whole
```

```python
import functools
import math

import jax
import jax.numpy as jnp
import numpy as np
from jax import lax
from jax.experimental import pallas as pl
from jax.experimental.pallas import tpu as pltpu
from jax.sharding import PartitionSpec as P

AXES = ("mirror", "rows", "cols")
F32 = jnp.float32
BF16 = jnp.bfloat16
SENT = (BF16, BF16)
SUB = 256
STRIP = 16
LAST = (((1,), (1,)), ((), ()))


class Plan:
    def __init__(self, pieces, half):
        self.pieces = pieces
        self.blocks = math.isqrt(4 * pieces)
        assert self.blocks * self.blocks == 4 * pieces and self.blocks % 4 == 0
        self.homes = self.blocks // 2
        self.per_half = pieces // self.blocks
        self.block_len = half // self.blocks
        self.piece_len = half // pieces
        self.tile = min(1024, self.block_len)
        self.tiles = self.block_len // self.tile

    def device(self, block, home):
        return home // self.per_half * self.pieces + block * self.per_half + home % self.per_half

    def route(self, near, step):
        pairs = []
        for block in range(self.blocks):
            for home in range(self.homes):
                other = block if near else (block + home + 1) % self.blocks
                source = self.device(other, (home + step) % self.homes)
                pairs.append((source, self.device(block, home)))
        return pairs

    def jobs(self):
        count = self.tiles
        pair = [(i, count + j) for i in range(count) for j in range(count)]
        diagonal = [
            (low + i, low + j) for low in (0, count) for i in range(count) for j in range(i + 1, count)
        ]
        tables = []
        for work in (pair, diagonal):
            table = np.zeros((3, count * count + 1), np.int32)
            for at, (i, j) in enumerate(work):
                table[:, at] = i, j, at == 0 or work[at - 1][0] != i
            tables.append(table)
        return tables[0], tables[1], len(pair), len(diagonal)


def operator_kernel(plan, table, counts, geo, *refs):
    pieces = refs[: plan.blocks]
    results = refs[plan.blocks : 2 * plan.blocks]
    drive, by_column, by_row, near, far, turned = refs[2 * plan.blocks :]
    tile, homes, piece_len = plan.tile, plan.homes, plan.piece_len
    chunks = tile // SUB
    strips = SUB // STRIP

    def place(index):
        home = lax.rem(counts[2] + index % homes, homes)
        half = home // plan.per_half
        offset = (index // homes) * plan.block_len + lax.rem(home, plan.per_half) * piece_len
        return half, pl.multiple_of(offset, 128)

    for index in range(plan.blocks):
        half, offset = place(index)
        value = pieces[index][...]
        drive[pl.ds(pl.multiple_of(half * 16, 16), 16), pl.ds(offset, piece_len)] = value
        drive[pl.ds(pl.multiple_of(48 - half * 16, 16), 16), pl.ds(offset, piece_len)] = value
    by_column[...] = jnp.zeros_like(by_column)
    by_row[...] = jnp.zeros_like(by_row)

    def turn(row0):
        for part in range(tile // 128):
            turned[part * 128 : part * 128 + 128, :] = jnp.transpose(geo[:, pl.ds(row0 + part * 128, 128)])

    def make(slot, row, col0, first, at, lanes=0):
        part = turned[row : row + STRIP, :]
        x_r, y_r, z_r, q_r = [jnp.broadcast_to(part[:, n : n + 1], (STRIP, 128)) for n in range(4)]
        for lane in range(lanes, tile, 128):
            cols = geo[:, pl.ds(col0 + lane, 128)]
            diff_x = x_r - cols[0:1]
            diff_z = z_r - cols[2:3]
            base = (q_r + cols[3:4]) + diff_x * diff_x + diff_z * diff_z
            cross = y_r * cols[4:5]
            near[slot, at : at + STRIP, lane : lane + 128] = lax.rsqrt(base - cross).astype(BF16)
            far[slot, at : at + STRIP, lane : lane + 128] = lax.rsqrt(base + cross).astype(BF16)

    def to_columns(slot, row0, col0, chunk):
        lanes = slice(chunk * SUB, chunk * SUB + SUB)
        rows = pl.ds(row0, SUB)
        by_column[:, pl.ds(col0 + chunk * SUB, SUB)] += jnp.dot(
            drive[0:32, rows], near[slot, :, lanes], preferred_element_type=F32
        ) + jnp.dot(drive[32:64, rows], far[slot, :, lanes], preferred_element_type=F32)

    def to_rows(slot, col0, chunk):
        lanes = slice(chunk * SUB, chunk * SUB + SUB)
        cols = pl.ds(col0 + chunk * SUB, SUB)
        return lax.dot_general(
            drive[0:32, cols], near[slot, :, lanes], LAST, preferred_element_type=F32
        ) + lax.dot_general(drive[32:64, cols], far[slot, :, lanes], LAST, preferred_element_type=F32)

    def pair_tile(at, carry):
        row0 = pl.multiple_of(table[0, at] * tile, tile)
        col0 = pl.multiple_of(table[1, at] * tile, tile)
        next0 = pl.multiple_of(table[1, at + 1] * tile, tile)

        @pl.when(table[2, at] == 1)
        def _():
            turn(row0)
            for strip in range(strips):
                make(0, strip * STRIP, col0, True, strip * STRIP)

        for sub in range(chunks):
            ahead, ahead0 = (sub + 1, col0) if sub + 1 < chunks else (0, next0)
            total = None
            for chunk in range(chunks):
                for strip in range(chunk * strips // chunks, (chunk + 1) * strips // chunks):
                    make((sub + 1) % 2, ahead * SUB + strip * STRIP, ahead0, False, strip * STRIP)
                to_columns(sub % 2, row0 + sub * SUB, col0, chunk)
                term = to_rows(sub % 2, col0, chunk)
                total = term if total is None else total + term
            by_row[:, pl.ds(row0 + sub * SUB, SUB)] += total
        return carry

    def diagonal_tile(at, carry):
        row0 = pl.multiple_of(at * tile, tile)
        turn(row0)
        for sub in range(chunks):
            slot = sub % 2
            for strip in range(strips):
                make(slot, sub * SUB + strip * STRIP, row0, False, strip * STRIP, sub * SUB)
            total = None
            for chunk in range(sub, chunks):
                to_columns(slot, row0 + sub * SUB, row0, chunk)
                if chunk > sub:
                    term = to_rows(slot, row0, chunk)
                    total = term if total is None else total + term
            if total is not None:
                by_row[:, pl.ds(row0 + sub * SUB, SUB)] += total
        return carry

    lax.fori_loop(0, counts[0], pair_tile, 0)
    lax.fori_loop(0, counts[1], diagonal_tile, 0)

    for index in range(plan.blocks):
        half, offset = place(index)
        rows = pl.ds(pl.multiple_of(half * 16, 16), 16)
        cols = pl.ds(offset, piece_len)
        results[index][...] = (by_column[rows, cols] + by_row[rows, cols]).astype(results[index].dtype)


def apply_operator(plan, table, counts, geo, pieces, sent):
    cells = 2 * plan.block_len
    vmem = pl.BlockSpec(memory_space=pltpu.VMEM)
    smem = pl.BlockSpec(memory_space=pltpu.SMEM)
    return pl.pallas_call(
        functools.partial(operator_kernel, plan),
        in_specs=[smem, smem, vmem] + [vmem] * plan.blocks,
        out_specs=[vmem] * plan.blocks,
        out_shape=[
            jax.ShapeDtypeStruct((16, plan.piece_len), sent if index else F32) for index in range(plan.blocks)
        ],
        scratch_shapes=[
            pltpu.VMEM((64, cells), BF16),
            pltpu.VMEM((32, cells), F32),
            pltpu.VMEM((32, cells), F32),
            pltpu.VMEM((2, SUB, plan.tile), BF16),
            pltpu.VMEM((2, SUB, plan.tile), BF16),
            pltpu.VMEM((plan.tile, 8), F32),
        ],
        compiler_params=pltpu.CompilerParams(vmem_limit_bytes=40 * 2**20),
        name="peec_pairs",
    )(table, counts, geo, *pieces)


def gather_pieces(plan, own):
    pieces = [own]
    for step in range(1, plan.homes):
        pieces.append(lax.ppermute(own, AXES, plan.route(True, step)))
    for step in range(plan.homes):
        pieces.append(lax.ppermute(own, AXES, plan.route(False, step)))
    return pieces


def return_pieces(plan, partials):
    total = partials[0]
    for index in range(1, plan.blocks):
        route = plan.route(index < plan.homes, index % plan.homes)
        back = [(target, source) for source, target in route]
        total = total + lax.ppermute(partials[index], AXES, back).astype(F32)
    return total


def local_geometry(plan, geometry, block, partner):
    scale = math.sqrt(2 * geometry.shape[1])
    length = plan.block_len
    cells = jnp.concatenate(
        [lax.dynamic_slice_in_dim(geometry, at * length, length, 1) for at in (block, partner)], axis=1
    )
    x, y, z, size = [cells[n] * scale for n in range(4)]
    zero = jnp.zeros_like(x)
    return jnp.stack([x, y, z, y * y + size * size, y + y, zero, zero, zero])


def on_device(plan, currents, right_side, geometry):
    piece = lax.axis_index("rows") * lax.axis_size("cols") + lax.axis_index("cols")
    block = piece // plan.per_half
    home = lax.axis_index("mirror") * plan.per_half + piece % plan.per_half
    partner = (block + home + 1) % plan.blocks
    pair, diagonal, pair_count, diagonal_count = plan.jobs()
    on_diagonal = (home == plan.homes - 1) & (block >= plan.homes)
    table = jnp.where(on_diagonal, diagonal, pair)
    counts = jnp.stack(
        [
            jnp.where(on_diagonal, diagonal_count, pair_count),
            jnp.where(on_diagonal, 2 * plan.tiles, 0),
            home,
        ]
    ).astype(jnp.int32)
    geo = local_geometry(plan, geometry, block, partner)

    own = lax.dynamic_slice_in_dim(currents, lax.axis_index("cols") * plan.piece_len, plan.piece_len, 1)
    partials = apply_operator(plan, table, counts, geo, gather_pieces(plan, own), SENT[0])
    residual = right_side - return_pieces(plan, partials)
    pieces = gather_pieces(plan, residual.astype(BF16))
    partials = apply_operator(plan, table, counts, geo, pieces, SENT[1])
    return residual, return_pieces(plan, partials)


def solution(mesh):
    pieces = mesh.shape["rows"] * mesh.shape["cols"]

    def whole(currents, right_side, geometry):
        plan = Plan(pieces, geometry.shape[1])
        return jax.shard_map(
            functools.partial(on_device, plan),
            mesh=mesh,
            in_specs=(P(None, ("mirror", "rows")), P(None, AXES), P()),
            out_specs=(P(None, AXES), P(None, AXES)),
            check_vma=False,
        )(currents, right_side, geometry)

    return whole
```

```python
import functools
import math

import jax
import jax.numpy as jnp
import numpy as np
from jax import lax
from jax.experimental import pallas as pl
from jax.experimental.pallas import tpu as pltpu
from jax.sharding import PartitionSpec as P

AXES = ("mirror", "rows", "cols")
F32 = jnp.float32
BF16 = jnp.bfloat16
SENT = (BF16, BF16)
SUB = 256
STRIP = 16
LAST = (((1,), (1,)), ((), ()))


class Plan:
    def __init__(self, pieces, half):
        self.pieces = pieces
        self.blocks = math.isqrt(4 * pieces)
        assert self.blocks * self.blocks == 4 * pieces and self.blocks % 4 == 0
        self.homes = self.blocks // 2
        self.per_half = pieces // self.blocks
        self.block_len = half // self.blocks
        self.piece_len = half // pieces
        self.tile = min(1024, self.block_len)
        self.tiles = self.block_len // self.tile

    def device(self, block, home):
        return home // self.per_half * self.pieces + block * self.per_half + home % self.per_half

    def route(self, near, step):
        pairs = []
        for block in range(self.blocks):
            for home in range(self.homes):
                other = block if near else (block + home + 1) % self.blocks
                source = self.device(other, (home + step) % self.homes)
                pairs.append((source, self.device(block, home)))
        return pairs

    def jobs(self):
        count = self.tiles
        pair = [(i, count + j) for i in range(count) for j in range(count)]
        diagonal = [
            (low + i, low + j) for low in (0, count) for i in range(count) for j in range(i + 1, count)
        ]
        tables = []
        for work in (pair, diagonal):
            table = np.zeros((2, count * count + 1), np.int32)
            for at, place in enumerate(work):
                table[:, at] = place
            tables.append(table)
        return tables[0], tables[1], len(pair), len(diagonal)


def operator_kernel(plan, table, counts, geo, *refs):
    pieces = refs[: plan.blocks]
    results = refs[plan.blocks : 2 * plan.blocks]
    drive, by_column, by_row, near, far, turned = refs[2 * plan.blocks :]
    tile, homes, piece_len = plan.tile, plan.homes, plan.piece_len
    chunks = tile // SUB
    strips = SUB // STRIP

    def place(index):
        home = lax.rem(counts[2] + index % homes, homes)
        half = home // plan.per_half
        offset = (index // homes) * plan.block_len + lax.rem(home, plan.per_half) * piece_len
        return half, pl.multiple_of(offset, 128)

    for index in range(plan.blocks):
        half, offset = place(index)
        value = pieces[index][...]
        drive[pl.ds(pl.multiple_of(half * 16, 16), 16), pl.ds(offset, piece_len)] = value
        drive[pl.ds(pl.multiple_of(48 - half * 16, 16), 16), pl.ds(offset, piece_len)] = value
    by_column[...] = jnp.zeros_like(by_column)
    by_row[...] = jnp.zeros_like(by_row)

    def turn(at, carry):
        row0 = pl.multiple_of(at * tile, tile)
        for part in range(tile // 128):
            turned[pl.ds(row0 + part * 128, 128), :] = jnp.transpose(geo[:, pl.ds(row0 + part * 128, 128)])
        return carry

    def make(slot, row, col0, at, lanes=0):
        part = turned[pl.ds(row, STRIP), :]
        x_r, y_r, z_r, q_r = [jnp.broadcast_to(part[:, n : n + 1], (STRIP, 128)) for n in range(4)]
        for lane in range(lanes, tile, 128):
            cols = geo[:, pl.ds(col0 + lane, 128)]
            diff_x = x_r - cols[0:1]
            diff_z = z_r - cols[2:3]
            base = (q_r + cols[3:4]) + diff_x * diff_x + diff_z * diff_z
            cross = y_r * cols[4:5]
            near[slot, at : at + STRIP, lane : lane + 128] = lax.rsqrt(base - cross).astype(BF16)
            far[slot, at : at + STRIP, lane : lane + 128] = lax.rsqrt(base + cross).astype(BF16)

    def to_columns(slot, row0, col0, chunk):
        lanes = slice(chunk * SUB, chunk * SUB + SUB)
        rows = pl.ds(row0, SUB)
        by_column[:, pl.ds(col0 + chunk * SUB, SUB)] += jnp.dot(
            drive[0:32, rows], near[slot, :, lanes], preferred_element_type=F32
        ) + jnp.dot(drive[32:64, rows], far[slot, :, lanes], preferred_element_type=F32)

    def to_rows(slot, col0, chunk):
        lanes = slice(chunk * SUB, chunk * SUB + SUB)
        cols = pl.ds(col0 + chunk * SUB, SUB)
        return lax.dot_general(
            drive[0:32, cols], near[slot, :, lanes], LAST, preferred_element_type=F32
        ) + lax.dot_general(drive[32:64, cols], far[slot, :, lanes], LAST, preferred_element_type=F32)

    def pair_tile(at, carry):
        row0 = pl.multiple_of(table[0, at] * tile, tile)
        col0 = pl.multiple_of(table[1, at] * tile, tile)
        next_row0 = pl.multiple_of(table[0, at + 1] * tile, tile)
        next_col0 = pl.multiple_of(table[1, at + 1] * tile, tile)
        for sub in range(chunks):
            inside = sub + 1 < chunks
            ahead_row, ahead_col = (row0 + (sub + 1) * SUB, col0) if inside else (next_row0, next_col0)
            total = None
            for chunk in range(chunks):
                for strip in range(chunk * strips // chunks, (chunk + 1) * strips // chunks):
                    make((sub + 1) % 2, ahead_row + strip * STRIP, ahead_col, strip * STRIP)
                to_columns(sub % 2, row0 + sub * SUB, col0, chunk)
                term = to_rows(sub % 2, col0, chunk)
                total = term if total is None else total + term
            by_row[:, pl.ds(row0 + sub * SUB, SUB)] += total
        return carry

    def diagonal_tile(at, carry):
        row0 = pl.multiple_of(at * tile, tile)
        for sub in range(chunks):
            slot = sub % 2
            for strip in range(strips):
                make(slot, row0 + sub * SUB + strip * STRIP, row0, strip * STRIP, sub * SUB)
            total = None
            for chunk in range(sub, chunks):
                to_columns(slot, row0 + sub * SUB, row0, chunk)
                if chunk > sub:
                    term = to_rows(slot, row0, chunk)
                    total = term if total is None else total + term
            if total is not None:
                by_row[:, pl.ds(row0 + sub * SUB, SUB)] += total
        return carry

    lax.fori_loop(0, jnp.maximum(plan.tiles, counts[1]), turn, 0)
    first_row = pl.multiple_of(table[0, 0] * tile, tile)
    first_col = pl.multiple_of(table[1, 0] * tile, tile)
    for strip in range(strips):
        make(0, first_row + strip * STRIP, first_col, strip * STRIP)
    lax.fori_loop(0, counts[0], pair_tile, 0)
    lax.fori_loop(0, counts[1], diagonal_tile, 0)

    for index in range(plan.blocks):
        half, offset = place(index)
        rows = pl.ds(pl.multiple_of(half * 16, 16), 16)
        cols = pl.ds(offset, piece_len)
        results[index][...] = (by_column[rows, cols] + by_row[rows, cols]).astype(results[index].dtype)


def apply_operator(plan, table, counts, geo, pieces, sent):
    cells = 2 * plan.block_len
    vmem = pl.BlockSpec(memory_space=pltpu.VMEM)
    smem = pl.BlockSpec(memory_space=pltpu.SMEM)
    return pl.pallas_call(
        functools.partial(operator_kernel, plan),
        in_specs=[smem, smem, vmem] + [vmem] * plan.blocks,
        out_specs=[vmem] * plan.blocks,
        out_shape=[
            jax.ShapeDtypeStruct((16, plan.piece_len), sent if index else F32) for index in range(plan.blocks)
        ],
        scratch_shapes=[
            pltpu.VMEM((64, cells), BF16),
            pltpu.VMEM((32, cells), F32),
            pltpu.VMEM((32, cells), F32),
            pltpu.VMEM((2, SUB, plan.tile), BF16),
            pltpu.VMEM((2, SUB, plan.tile), BF16),
            pltpu.VMEM((cells, 8), F32),
        ],
        compiler_params=pltpu.CompilerParams(vmem_limit_bytes=40 * 2**20),
        name="peec_pairs",
    )(table, counts, geo, *pieces)


def gather_pieces(plan, own):
    pieces = [own]
    for step in range(1, plan.homes):
        pieces.append(lax.ppermute(own, AXES, plan.route(True, step)))
    for step in range(plan.homes):
        pieces.append(lax.ppermute(own, AXES, plan.route(False, step)))
    return pieces


def return_pieces(plan, partials):
    total = partials[0]
    for index in range(1, plan.blocks):
        route = plan.route(index < plan.homes, index % plan.homes)
        back = [(target, source) for source, target in route]
        total = total + lax.ppermute(partials[index], AXES, back).astype(F32)
    return total


def local_geometry(plan, geometry, block, partner):
    scale = math.sqrt(2 * geometry.shape[1])
    length = plan.block_len
    cells = jnp.concatenate(
        [lax.dynamic_slice_in_dim(geometry, at * length, length, 1) for at in (block, partner)], axis=1
    )
    x, y, z, size = [cells[n] * scale for n in range(4)]
    zero = jnp.zeros_like(x)
    return jnp.stack([x, y, z, y * y + size * size, y + y, zero, zero, zero])


def on_device(plan, currents, right_side, geometry):
    piece = lax.axis_index("rows") * lax.axis_size("cols") + lax.axis_index("cols")
    block = piece // plan.per_half
    home = lax.axis_index("mirror") * plan.per_half + piece % plan.per_half
    partner = (block + home + 1) % plan.blocks
    pair, diagonal, pair_count, diagonal_count = plan.jobs()
    on_diagonal = (home == plan.homes - 1) & (block >= plan.homes)
    table = jnp.where(on_diagonal, diagonal, pair)
    counts = jnp.stack(
        [
            jnp.where(on_diagonal, diagonal_count, pair_count),
            jnp.where(on_diagonal, 2 * plan.tiles, 0),
            home,
        ]
    ).astype(jnp.int32)
    geo = local_geometry(plan, geometry, block, partner)

    own = lax.dynamic_slice_in_dim(currents, lax.axis_index("cols") * plan.piece_len, plan.piece_len, 1)
    partials = apply_operator(plan, table, counts, geo, gather_pieces(plan, own), SENT[0])
    residual = right_side - return_pieces(plan, partials)
    pieces = gather_pieces(plan, residual.astype(BF16))
    partials = apply_operator(plan, table, counts, geo, pieces, SENT[1])
    return residual, return_pieces(plan, partials)


def solution(mesh):
    pieces = mesh.shape["rows"] * mesh.shape["cols"]

    def whole(currents, right_side, geometry):
        plan = Plan(pieces, geometry.shape[1])
        return jax.shard_map(
            functools.partial(on_device, plan),
            mesh=mesh,
            in_specs=(P(None, ("mirror", "rows")), P(None, AXES), P()),
            out_specs=(P(None, AXES), P(None, AXES)),
            check_vma=False,
        )(currents, right_side, geometry)

    return whole
```
